256 devices in a mesh: ctx: 32 (over y, z), kvh: 8 (over x, core).
Axes of the slice: x: 4, y: 4, z: 8, core: 2. Of those that a mesh axis runs over, the one named last changes fastest.
Arguments:
- queries: bfloat16 [65536, 4096], P('ctx', 'kvh'), may hold values from -64 to 64
- keys: bfloat16 [65536, 1024], P('ctx', 'kvh'), may hold values from -4 to 4
- values: bfloat16 [65536, 1024], P('ctx', 'kvh'), may hold values from -6 to 6
- vertical: int32 [32, 512], P('kvh'), may hold values from 0 to 65535, as said below
Outputs:
- attended: bfloat16 [65536, 4096], P('ctx', 'kvh')
The draws below stay inside these ranges and needn't reach their ends.
Inputs may be any that keep to these rules, and one draw needn't show every extreme that they name: `vertical`: each row holds 512 distinct positions in rising order; at most 32 of a row lie among the 2048 tokens of one device, and exactly 32 do for one device in every row.
All inputs are finite; a program needn't handle non-finite values.
Results may differ from the reference program's by a relative error of at most 0.0046.
Values may be sent and summed in bfloat16 or wider, within the bound.
No kernel may reach another device: no remote copies, remote signals or barrier semaphores. Data moves between devices by JAX's collectives and lax.ppermute only.
A program may use at most 64 MiB of HBM per device.

```python
import math
import jax
import jax.numpy as jnp
from jax import lax

TOK_DEV = 2048
HEAD = 128
Q_PER_KV = 4
V_COLS = 512
BAND = 1024
TOKENS = 65536
KV_HEADS = 8
HEADS = 32
COL_CAP = 32
N_CTX = 32


def draw_keys(key, part):
    key = jax.random.fold_in(key, 11)
    raw = jax.random.normal(key, (TOKENS, KV_HEADS * HEAD), jnp.float32)
    return jnp.clip(raw, -4.0, 4.0).astype(jnp.bfloat16)


def draw_queries(key, part):
    key = jax.random.fold_in(key, 12)
    raw = jax.random.normal(key, (TOKENS, HEADS * HEAD), jnp.float32)
    return jnp.clip(raw, -6.0, 6.0).astype(jnp.bfloat16)


def draw_vertical(key, part):
    key = jax.random.fold_in(key, 7)

    def one_head(head_key):
        pos_key, order_key, pick_key = jax.random.split(head_key, 3)
        block_keys = jax.random.split(pos_key, N_CTX)
        inner = jax.vmap(lambda kk: jax.random.permutation(kk, TOK_DEV)[:COL_CAP])(block_keys)
        spots = inner + (jnp.arange(N_CTX) * TOK_DEV)[:, None]
        order = jax.random.permutation(order_key, N_CTX)
        spots = spots[order]
        full_block = spots[0]
        rest = spots[1:].reshape(-1)
        chosen = jax.random.permutation(pick_key, rest.shape[0])[:V_COLS - COL_CAP]
        columns = jnp.concatenate([full_block, rest[chosen]])
        return jnp.sort(columns)
    head_keys = jax.random.split(key, HEADS)
    return jax.vmap(one_head)(head_keys).astype(jnp.int32)


def block_scale(own_key, dims, shards, smallest, top_value):
    def one(dim, shards_of):
        draws = jax.random.uniform(jax.random.fold_in(jax.random.fold_in(own_key, 6), dim), (shards_of,), jnp.float32, smallest / len(shards), top_value / len(shards))
        return jnp.repeat(jnp.exp(draws), dims[dim] // shards_of).reshape((-1,) + (1,) * (len(dims) - dim - 1))

    factor_of = one(*shards[0])
    for cut in shards[1:]:
        factor_of = factor_of * one(*cut)
    return factor_of


def noise(rng, extent, width, most, shards=(), kind=jnp.bfloat16):
    entries = width * jax.random.normal(rng, extent, jnp.float32)
    if shards:
        entries = entries * block_scale(rng, extent, shards, -0.22, 0.18)
    return jnp.clip(entries, -most, most).astype(kind)


def setup_inputs(seed: int = 0) -> dict:
    arg_keys = jax.random.split(jax.random.key(seed), 5)
    return {
        "queries": draw_queries(jax.random.fold_in(arg_keys[4], 71), 0),
        "keys": draw_keys(jax.random.fold_in(arg_keys[4], 71), 0),
        "values": noise(arg_keys[2], (TOKENS, KV_HEADS * HEAD), 1.0, 6.0, ((0, 32), (1, 8))),
        "vertical": draw_vertical(jax.random.fold_in(arg_keys[4], 71), 0),
    }


def attend(qblk, band_k, band_v, band_pos, vert_k, vert_v, vert_pos, qpos):
    scale = 1.0 / math.sqrt(qblk.shape[-1])
    q32 = qblk.astype(jnp.float32)
    band_s = jnp.einsum('qhd,kd->hqk', q32, band_k.astype(jnp.float32)) * scale
    vert_s = jnp.einsum('qhd,hcd->hqc', q32, vert_k.astype(jnp.float32)) * scale
    band_ok = (band_pos[None, :] <= qpos[:, None]) & (band_pos[None, :] > qpos[:, None] - BAND) & (band_pos[None, :] >= 0)
    vert_ok = vert_pos[:, None, :] <= qpos[None, :, None] - BAND
    band_s = jnp.where(band_ok[None, :, :], band_s, -1e+30)
    vert_s = jnp.where(vert_ok, vert_s, -1e+30)
    scores = jnp.concatenate([vert_s, band_s], -1)
    top = lax.optimization_barrier(jnp.max(scores, -1, keepdims=True))
    expo = jnp.exp(scores - top)
    total = lax.optimization_barrier(jnp.sum(expo, -1))
    weight = expo.astype(jnp.bfloat16).astype(jnp.float32)
    ncols = vert_k.shape[1]
    out = jnp.einsum('hqc,hcd->qhd', weight[:, :, :ncols], vert_v.astype(jnp.float32))
    out = out + jnp.einsum('hqk,kd->qhd', weight[:, :, ncols:], band_v.astype(jnp.float32))
    out = out / jnp.transpose(total)[:, :, None]
    return out.astype(jnp.bfloat16).reshape(qblk.shape[0], -1)

def reference(queries, keys, values, vertical):
    group = Q_PER_KV
    block = min(512, TOK_DEV)
    q_all = queries.reshape(TOKENS, KV_HEADS, group, HEAD).transpose(1, 0, 2, 3)
    k_all = keys.reshape(TOKENS, KV_HEADS, HEAD).transpose(1, 0, 2)
    v_all = values.reshape(TOKENS, KV_HEADS, HEAD).transpose(1, 0, 2)
    c_all = vertical.reshape(KV_HEADS, group, V_COLS)

    def one_group(items):
        q_grp, k_grp, v_grp, c_grp = items
        vert_k = jnp.take(k_grp, c_grp, axis=0)
        vert_v = jnp.take(v_grp, c_grp, axis=0)
        padding = jnp.zeros((BAND, HEAD), k_grp.dtype)
        k_pad = jnp.concatenate([padding, k_grp], 0)
        v_pad = jnp.concatenate([padding, v_grp], 0)

        def one_block(start):
            qblk = lax.dynamic_slice_in_dim(q_grp, start, block, 0)
            band_k = lax.dynamic_slice_in_dim(k_pad, start, BAND + block, 0)
            band_v = lax.dynamic_slice_in_dim(v_pad, start, BAND + block, 0)
            band_pos = start - BAND + jnp.arange(BAND + block, dtype=jnp.int32)
            qpos = start + jnp.arange(block, dtype=jnp.int32)
            return attend(qblk, band_k, band_v, band_pos, vert_k, vert_v, c_grp, qpos)
        starts = jnp.arange(TOKENS // block, dtype=jnp.int32) * block
        return lax.map(one_block, starts).reshape(TOKENS, group * HEAD)
    result = lax.map(one_group, (q_all, k_all, v_all, c_all))
    return result.transpose(1, 0, 2).reshape(TOKENS, KV_HEADS * group * HEAD)
```

```python
import math
import jax
import jax.numpy as jnp
from jax import lax
from jax.experimental import pallas as pl
from jax.experimental.pallas import tpu as pltpu
from jax.sharding import PartitionSpec as P
TOK=2048; HEAD=128; GROUP=4; COLS=512; BAND=1024; CAP=32; NCTX=32
QB=256
C=math.log2(math.e)/math.sqrt(HEAD)
F32=jnp.float32; BF=jnp.bfloat16
NEG=-1e30

def dot(a,b): return jnp.dot(a,b,preferred_element_type=F32)

def pick_kernel(base_ref, vert_ref, k_ref, v_ref, out_ref):
    base=base_ref[0]
    vert=vert_ref[...]
    cols=lax.broadcasted_iota(jnp.int32,(CAP,COLS),1)
    slot=lax.broadcasted_iota(jnp.int32,(CAP,COLS),0)
    toks=lax.broadcasted_iota(jnp.int32,(CAP,TOK),1)
    rows=[]
    for h in range(GROUP):
        v=vert[h:h+1,:]-base
        start=jnp.sum((v<0).astype(jnp.int32),axis=1,keepdims=True)
        hit=(cols-start==slot)&(v<TOK)
        pos=jnp.sum(jnp.where(hit,v+1,0),axis=1,keepdims=True)-1
        rows.append((toks==pos).astype(F32).astype(BF))
    sel=jnp.concatenate(rows,0)
    out_ref[:,:HEAD]=dot(sel,k_ref[...]).astype(BF)
    out_ref[:,HEAD:]=dot(sel,v_ref[...]).astype(BF)

def pick(base,vertical,keys,values):
    return pl.pallas_call(pick_kernel,
        out_shape=jax.ShapeDtypeStruct((GROUP*CAP,2*HEAD),BF),
        in_specs=[pl.BlockSpec(memory_space=pltpu.SMEM)]+[pl.BlockSpec(memory_space=pltpu.VMEM)]*3,
        out_specs=pl.BlockSpec(memory_space=pltpu.VMEM),
        compiler_params=pltpu.CompilerParams(vmem_limit_bytes=16<<20),
        name="pick")(base,vertical,keys,values)

def band_kernel(first_ref, q_ref, k0_ref, k1_ref, v0_ref, v1_ref, acc_ref, ml_ref, kt, vx):
    step=pl.program_id(0)
    @pl.when(step==0)
    def _():
        first=first_ref[0]!=0
        k0=jnp.where(first,jnp.broadcast_to(k1_ref[0:1,:],k0_ref.shape),k0_ref[...])
        kt[:,:BAND]=k0.T
        kt[:,BAND:]=k1_ref[...].T
        one=jnp.ones((BAND,HEAD),BF)
        zero=jnp.zeros((BAND,HEAD),BF)
        vx[:BAND,:HEAD]=jnp.where(first,zero,v0_ref[...])
        vx[:BAND,HEAD:]=jnp.where(first,zero,one)
        vx[BAND:,:HEAD]=v1_ref[...]
        vx[BAND:,HEAD:]=one
    off=pl.multiple_of(step*QB,QB)
    tri=lax.broadcasted_iota(jnp.int32,(QB,QB),1)<=lax.broadcasted_iota(jnp.int32,(QB,QB),0)
    lane=lax.broadcasted_iota(jnp.int32,(QB,HEAD),1)
    ml=jnp.zeros((QB,HEAD),F32)
    for h in range(GROUP):
        q=q_ref[:,h*HEAD:(h+1)*HEAD]
        s=dot(q,kt[:,pl.ds(off,BAND+QB)])
        s_in=s[:,QB:BAND]
        s_edge=jnp.where(tri,s[:,BAND:],s[:,:QB])
        m=jnp.maximum(jnp.max(s_in,axis=1,keepdims=True),jnp.max(s_edge,axis=1,keepdims=True))
        p_in=jnp.exp2((s_in-m)*C).astype(BF)
        p_edge=jnp.exp2((s_edge-m)*C)
        p_last=jnp.where(tri,p_edge,0.0).astype(BF)
        p_first=jnp.where(tri,0.0,p_edge).astype(BF)
        p=jnp.concatenate([p_first,p_in,p_last],1)
        o=dot(p,vx[pl.ds(off,BAND+QB),:])
        acc_ref[:,h*HEAD:(h+1)*HEAD]=o[:,:HEAD]
        ml=jnp.where(lane==h,m,jnp.where(lane==GROUP+h,o[:,HEAD:],ml))
    ml_ref[...]=ml

def band(first,queries,qhalf,k0,k1,v0,v1,bk0,bk1):
    n=BAND//QB
    kspec=lambda b: pl.BlockSpec((BAND,HEAD),lambda i: (b,0))
    return pl.pallas_call(band_kernel,
        grid=(n,),
        out_shape=(jax.ShapeDtypeStruct((BAND,GROUP*HEAD),F32),jax.ShapeDtypeStruct((BAND,HEAD),F32)),
        in_specs=[pl.BlockSpec(memory_space=pltpu.SMEM),
            pl.BlockSpec((QB,GROUP*HEAD),lambda i:(qhalf*n+i,0)),kspec(bk0),kspec(bk1),kspec(bk0),kspec(bk1)],
        out_specs=(pl.BlockSpec((QB,GROUP*HEAD),lambda i:(i,0)),pl.BlockSpec((QB,HEAD),lambda i:(i,0))),
        scratch_shapes=[pltpu.VMEM((HEAD,2*BAND),BF),pltpu.VMEM((2*BAND,2*HEAD),BF)],
        compiler_params=pltpu.CompilerParams(vmem_limit_bytes=32<<20),
        cost_estimate=pl.CostEstimate(flops=4*BAND*GROUP*HEAD*(BAND+QB),bytes_accessed=6<<20,transcendentals=BAND*BAND*GROUP),
        name="band")(first,queries,k0,k1,v0,v1)

def vert_kernel(base_ref, q_ref, g_ref, vert_ref, vertt_ref, code_ref, a0_ref, ml0_ref, a1_ref, ml1_ref, out_ref, kt, vx):
    step=pl.program_id(0)
    @pl.when(step==0)
    def _():
        lanes=lax.broadcasted_iota(jnp.int32,(COLS,HEAD),1)
        rows=lax.broadcasted_iota(jnp.int32,(COLS,1),0)
        code=code_ref[...]
        for h in range(GROUP):
            v=vertt_ref[:,h:h+1]
            starts=jnp.sum((v<lanes*TOK).astype(jnp.int32),axis=0,keepdims=True)
            d=v//TOK
            start=jnp.sum(jnp.where(lanes==d,starts,0),axis=1,keepdims=True)
            mine=d*CAP+rows-start
            sel=(mine==code).astype(F32).astype(BF)
            t=dot(sel,g_ref[:,h*CAP:(h+1)*CAP,:].reshape(NCTX*CAP,2*HEAD))
            kt[h]=t[:,:HEAD].astype(BF).T
            vx[h,:,:HEAD]=t[:,HEAD:].astype(BF)
            vx[h,:,HEAD:]=jnp.ones((COLS,HEAD),BF)
    half=(TOK//QB)//2
    def body(a_ref,ml_ref):
        qpos=base_ref[0]+step*QB-BAND+lax.broadcasted_iota(jnp.int32,(QB,1),0)
        ml=ml_ref[...]
        for h in range(GROUP):
            s=dot(q_ref[:,h*HEAD:(h+1)*HEAD],kt[h])
            s=jnp.where(vert_ref[h:h+1,:]<=qpos,s,NEG)
            mb=ml[:,h:h+1]; lb=ml[:,GROUP+h:GROUP+h+1]
            m=jnp.maximum(jnp.max(s,axis=1,keepdims=True),mb)
            p=jnp.exp2((s-m)*C).astype(BF)
            o=dot(p,vx[h])
            alpha=jnp.exp2((mb-m)*C)
            num=a_ref[:,h*HEAD:(h+1)*HEAD]*alpha+o[:,:HEAD]
            den=o[:,HEAD:]+lb*alpha
            out_ref[:,h*HEAD:(h+1)*HEAD]=(num/den).astype(BF)
    @pl.when(step<half)
    def _(): body(a0_ref,ml0_ref)
    @pl.when(step>=half)
    def _(): body(a1_ref,ml1_ref)

def vert(base,queries,gathered,vertical,vertt,code,a0,ml0,a1,ml1):
    n=TOK//QB
    full=lambda *s: pl.BlockSpec(s,lambda i:(0,)*len(s))
    lo=lambda i:(jnp.minimum(i,n//2-1),0)
    hi=lambda i:(jnp.maximum(i-n//2,0),0)
    return pl.pallas_call(vert_kernel,
        grid=(n,),
        out_shape=jax.ShapeDtypeStruct((TOK,GROUP*HEAD),BF),
        in_specs=[pl.BlockSpec(memory_space=pltpu.SMEM),
            pl.BlockSpec((QB,GROUP*HEAD),lambda i:(i,0)),
            full(NCTX,GROUP*CAP,2*HEAD),full(GROUP,COLS),full(COLS,GROUP),full(1,NCTX*CAP),
            pl.BlockSpec((QB,GROUP*HEAD),lo),pl.BlockSpec((QB,HEAD),lo),
            pl.BlockSpec((QB,GROUP*HEAD),hi),pl.BlockSpec((QB,HEAD),hi)],
        out_specs=pl.BlockSpec((QB,GROUP*HEAD),lambda i:(i,0)),
        scratch_shapes=[pltpu.VMEM((GROUP,HEAD,COLS),BF),pltpu.VMEM((GROUP,COLS,2*HEAD),BF)],
        compiler_params=pltpu.CompilerParams(vmem_limit_bytes=40<<20),
        cost_estimate=pl.CostEstimate(flops=4*TOK*GROUP*HEAD*COLS,bytes_accessed=12<<20,transcendentals=TOK*COLS*GROUP),
        name="vert")(base,queries,gathered,vertical,vertt,code,a0,ml0,a1,ml1)


AXES = ("ctx", "kvh")


def hop(array, grid, step):
    ny, nz = grid
    nk = lax.axis_size("kvh")
    pairs = []
    for y in range(ny):
        for z in range(nz):
            for k in range(nk):
                s = 1 if k % 2 == 0 else -1
                to = ((y + s * step[0]) % ny) * nz + (z + s * step[1]) % nz
                pairs.append(((y * nz + z) * nk + k, to * nk + k))
    return lax.ppermute(array, AXES, pairs)


def widen(array, came, grid, steps):
    parts = [array] + [hop(array, grid, s) for s in steps]
    origin = list(came)
    for s in steps:
        origin += [(o[0] - s[0], o[1] - s[1]) for o in came]
    return jnp.concatenate(parts, 0), origin


def spread(own):
    grid = (4, 8)
    held, came = widen(own[None], [(0, 0)], grid, ((0, 2), (0, 4), (0, -2)))
    held, came = widen(held, came, grid, ((2, 0), (1, 1), (-1, 1)))
    even = held[:8]
    a = hop(even, grid, (1, 0))
    b = hop(even, grid, (0, 1))
    came = came + [(y - 1, z) for y, z in came[:8]] + [(y, z - 1) for y, z in came[:8]]
    return jnp.concatenate([held, a, b], 0), came


def shards(queries, keys, values, vertical):
    ctx = lax.axis_index("ctx")
    base = (ctx * TOK).astype(jnp.int32)[None]
    inner = jnp.zeros((1,), jnp.int32)
    first = (ctx == 0).astype(jnp.int32)[None]

    own = pick(base, vertical, keys, values)
    shift = [(i, i + 1) for i in range(NCTX - 1)]
    edge_k = lax.ppermute(keys[TOK - BAND :], "ctx", shift)
    edge_v = lax.ppermute(values[TOK - BAND :], "ctx", shift)
    gathered, came = spread(own)

    sign = 1 - 2 * (lax.axis_index("kvh") % 2)
    oy = jnp.asarray([o[0] for o in came], jnp.int32)
    oz = jnp.asarray([o[1] for o in came], jnp.int32)
    device = ((ctx // 8 + sign * oy) % 4) * 8 + (ctx % 8 + sign * oz) % 8
    code = (device[:, None] * CAP + jnp.arange(CAP, dtype=jnp.int32)[None, :]).reshape(1, -1)

    acc1, ml1 = band(inner, queries, 1, keys, keys, values, values, 0, 1)
    acc0, ml0 = band(first, queries, 0, edge_k, keys, edge_v, values, 0, 0)
    return vert(base, queries, gathered, vertical, vertical.T, code, acc0, ml0, acc1, ml1)


def solution(mesh):
    in_specs = (P("ctx", "kvh"), P("ctx", "kvh"), P("ctx", "kvh"), P("kvh", None))
    return jax.shard_map(shards, mesh=mesh, in_specs=in_specs, out_specs=P("ctx", "kvh"), check_vma=False)
```

```python
import math

import jax
import jax.numpy as jnp
from jax import lax
from jax.experimental import pallas as pl
from jax.experimental.pallas import tpu as pltpu
from jax.sharding import PartitionSpec as P

TOK = 2048
HEAD = 128
GROUP = 4
COLS = 512
BAND = 1024
CAP = 32
NCTX = 32
QB = 256
VR = HEAD + 16
C = math.log2(math.e) / math.sqrt(HEAD)
F32 = jnp.float32
BF = jnp.bfloat16
NEG = -1e30
LIMIT = 56 << 20


def dot(a, b):
    return jnp.dot(a, b, preferred_element_type=F32)


def dot_t(a, b):
    return lax.dot_general(a, b, (((1,), (1,)), ((), ())), preferred_element_type=F32)


def pick_kernel(base_ref, vert_ref, k_ref, v_ref, out_ref, edge_ref):
    base = base_ref[0]
    vert = vert_ref[...]
    cols = lax.broadcasted_iota(jnp.int32, (CAP, COLS), 1)
    slot = lax.broadcasted_iota(jnp.int32, (CAP, COLS), 0)
    toks = lax.broadcasted_iota(jnp.int32, (CAP, TOK), 1)
    rows = []
    for h in range(GROUP):
        v = vert[h : h + 1, :] - base
        start = jnp.sum((v < 0).astype(jnp.int32), axis=1, keepdims=True)
        hit = (cols - start == slot) & (v < TOK)
        pos = jnp.sum(jnp.where(hit, v + 1, 0), axis=1, keepdims=True) - 1
        rows.append((toks == pos).astype(F32).astype(BF))
    sel = jnp.concatenate(rows, 0)
    out_ref[0, :, :HEAD] = dot(sel, k_ref[...]).astype(BF)
    out_ref[0, :, HEAD:] = dot(sel, v_ref[...]).astype(BF)
    edge_ref[:BAND, :] = k_ref[TOK - BAND :, :]
    edge_ref[BAND:, :] = v_ref[TOK - BAND :, :]


def pick(base, vertical, keys, values):
    full = lambda *s: pl.BlockSpec(s, lambda i: (0,) * len(s))
    return pl.pallas_call(
        pick_kernel,
        grid=(1,),
        out_shape=(
            jax.ShapeDtypeStruct((1, GROUP * CAP, 2 * HEAD), BF),
            jax.ShapeDtypeStruct((2 * BAND, HEAD), BF),
        ),
        in_specs=[pl.BlockSpec(memory_space=pltpu.SMEM), full(GROUP, COLS), full(TOK, HEAD), full(TOK, HEAD)],
        out_specs=(full(1, GROUP * CAP, 2 * HEAD), full(2 * BAND, HEAD)),
        compiler_params=pltpu.CompilerParams(vmem_limit_bytes=LIMIT),
        name="pick",
    )(base, vertical, keys, values)


def band_kernel(first_ref, q_ref, k0_ref, k1_ref, v0_ref, v1_ref, acc_ref, ml_ref, kx, vt):
    step = pl.program_id(0)

    @pl.when(step == 0)
    def _():
        first = first_ref[0] != 0
        kx[:BAND, :] = jnp.where(first, jnp.broadcast_to(k1_ref[0:1, :], k0_ref.shape), k0_ref[...])
        kx[BAND:, :] = k1_ref[...]
        vt[:HEAD, :BAND] = jnp.where(first, jnp.zeros(v0_ref.shape, BF), v0_ref[...]).T
        vt[:HEAD, BAND:] = v1_ref[...].T
        one = jnp.ones((VR - HEAD, BAND), BF)
        vt[HEAD:, :BAND] = jnp.where(first, jnp.zeros_like(one), one)
        vt[HEAD:, BAND:] = one

    off = pl.multiple_of(step * QB, QB)
    tri = lax.broadcasted_iota(jnp.int32, (QB, QB), 0) <= lax.broadcasted_iota(jnp.int32, (QB, QB), 1)
    scores = lambda h: dot_t(kx[pl.ds(off, BAND + QB), :], q_ref[:, h * HEAD : (h + 1) * HEAD])
    nxt = scores(0)
    for h in range(GROUP):
        s = nxt
        if h + 1 < GROUP:
            nxt = scores(h + 1)
        s_in = s[QB:BAND]
        s_edge = jnp.where(tri, s[BAND:], s[:QB])
        m = jnp.maximum(jnp.max(s_in, axis=0, keepdims=True), jnp.max(s_edge, axis=0, keepdims=True))
        p_in = jnp.exp2((s_in - m) * C).astype(BF)
        p_edge = jnp.exp2((s_edge - m) * C)
        p_last = jnp.where(tri, p_edge, 0.0).astype(BF)
        p_first = jnp.where(tri, 0.0, p_edge).astype(BF)
        p = jnp.concatenate([p_first, p_in, p_last], 0)
        o = dot(vt[:, pl.ds(off, BAND + QB)], p)
        acc_ref[h * HEAD : (h + 1) * HEAD, :] = o[:HEAD]
        ml_ref[h : h + 1, :] = m
        ml_ref[GROUP + h : GROUP + h + 1, :] = o[HEAD : HEAD + 1]


def band(first, queries, qhalf, k0, k1, v0, v1, bk0, bk1, bv0, bv1):
    n = BAND // QB
    spec = lambda b: pl.BlockSpec((BAND, HEAD), lambda i: (b, 0))
    return pl.pallas_call(
        band_kernel,
        grid=(n,),
        out_shape=(
            jax.ShapeDtypeStruct((GROUP * HEAD, BAND), F32),
            jax.ShapeDtypeStruct((2 * GROUP, BAND), F32),
        ),
        in_specs=[
            pl.BlockSpec(memory_space=pltpu.SMEM),
            pl.BlockSpec((QB, GROUP * HEAD), lambda i: (qhalf * n + i, 0)),
            spec(bk0),
            spec(bk1),
            spec(bv0),
            spec(bv1),
        ],
        out_specs=(
            pl.BlockSpec((GROUP * HEAD, QB), lambda i: (0, i)),
            pl.BlockSpec((2 * GROUP, QB), lambda i: (0, i)),
        ),
        scratch_shapes=[pltpu.VMEM((2 * BAND, HEAD), BF), pltpu.VMEM((VR, 2 * BAND), BF)],
        compiler_params=pltpu.CompilerParams(vmem_limit_bytes=LIMIT),
        cost_estimate=pl.CostEstimate(
            flops=8 * BAND * GROUP * HEAD * (BAND + QB),
            bytes_accessed=5 << 20,
            transcendentals=BAND * BAND * GROUP,
        ),
        name="band",
    )(first, queries, k0, k1, v0, v1)


def vert_kernel(nparts, *refs):
    base_ref, q_ref = refs[:2]
    g_refs = refs[2 : 2 + nparts]
    vertt_ref, code_ref, a0_ref, ml0_ref, a1_ref, ml1_ref, out_ref, kx, vt = refs[2 + nparts :]
    step = pl.program_id(0)

    @pl.when(step == 0)
    def _():
        lanes = lax.broadcasted_iota(jnp.int32, (COLS, HEAD), 1)
        rows = lax.broadcasted_iota(jnp.int32, (COLS, 1), 0)
        for h in range(GROUP):
            v = vertt_ref[:, h : h + 1]
            starts = jnp.sum((v < lanes * TOK).astype(jnp.int32), axis=0, keepdims=True)
            d = v // TOK
            start = jnp.sum(jnp.where(lanes == d, starts, 0), axis=1, keepdims=True)
            mine = d * CAP + rows - start
            t = None
            at = 0
            for g in g_refs:
                n = g.shape[0] * CAP
                sel = (mine == code_ref[:, at : at + n]).astype(F32).astype(BF)
                at += n
                part = dot(sel, g[:, h * CAP : (h + 1) * CAP, :].reshape(n, 2 * HEAD))
                t = part if t is None else t + part
            kx[h] = t[:, :HEAD].astype(BF)
            vt[h, :HEAD, :] = t[:, HEAD:].astype(BF).T
            vt[h, HEAD:, :] = jnp.ones((VR - HEAD, COLS), BF)

    half = (TOK // QB) // 2
    qpos = base_ref[0] + step * QB - BAND + lax.broadcasted_iota(jnp.int32, (1, QB), 1)

    def body(a_ref, ml_ref):
        scores = lambda h: dot_t(kx[h], q_ref[:, h * HEAD : (h + 1) * HEAD])
        nxt = scores(0)
        for h in range(GROUP):
            s = nxt
            if h + 1 < GROUP:
                nxt = scores(h + 1)
            s = jnp.where(vertt_ref[:, h : h + 1] <= qpos, s, NEG)
            mb = ml_ref[h : h + 1, :]
            lb = ml_ref[GROUP + h : GROUP + h + 1, :]
            m = jnp.maximum(jnp.max(s, axis=0, keepdims=True), mb)
            p = jnp.exp2((s - m) * C).astype(BF)
            o = dot(vt[h], p)
            alpha = jnp.exp2((mb - m) * C)
            den = o[HEAD : HEAD + 1] + lb * alpha
            num = a_ref[h * HEAD : (h + 1) * HEAD, :] * alpha + o[:HEAD]
            out_ref[:, h * HEAD : (h + 1) * HEAD] = (num * (1.0 / den)).T.astype(BF)

    @pl.when(step < half)
    def _():
        body(a0_ref, ml0_ref)

    @pl.when(step >= half)
    def _():
        body(a1_ref, ml1_ref)


def vert(base, queries, parts, vertt, code, a0, ml0, a1, ml1):
    n = TOK // QB
    full = lambda *s: pl.BlockSpec(s, lambda i: (0,) * len(s))
    lo = lambda i: (0, jnp.minimum(i, n // 2 - 1))
    hi = lambda i: (0, jnp.maximum(i - n // 2, 0))
    return pl.pallas_call(
        lambda *refs: vert_kernel(len(parts), *refs),
        grid=(n,),
        out_shape=jax.ShapeDtypeStruct((TOK, GROUP * HEAD), BF),
        in_specs=[
            pl.BlockSpec(memory_space=pltpu.SMEM),
            pl.BlockSpec((QB, GROUP * HEAD), lambda i: (i, 0)),
            *[full(*p.shape) for p in parts],
            full(COLS, GROUP),
            full(1, NCTX * CAP),
            pl.BlockSpec((GROUP * HEAD, QB), lo),
            pl.BlockSpec((2 * GROUP, QB), lo),
            pl.BlockSpec((GROUP * HEAD, QB), hi),
            pl.BlockSpec((2 * GROUP, QB), hi),
        ],
        out_specs=pl.BlockSpec((QB, GROUP * HEAD), lambda i: (i, 0)),
        scratch_shapes=[pltpu.VMEM((GROUP, COLS, HEAD), BF), pltpu.VMEM((GROUP, VR, COLS), BF)],
        compiler_params=pltpu.CompilerParams(vmem_limit_bytes=LIMIT),
        cost_estimate=pl.CostEstimate(
            flops=8 * TOK * GROUP * HEAD * COLS,
            bytes_accessed=12 << 20,
            transcendentals=TOK * COLS * GROUP,
        ),
        name="vert",
    )(base, queries, *parts, vertt, code, a0, ml0, a1, ml1)


AXES = ("ctx", "kvh")


def hop(array, grid, step):
    ny, nz = grid
    nk = lax.axis_size("kvh")
    pairs = []
    for y in range(ny):
        for z in range(nz):
            for k in range(nk):
                s = 1 if k % 2 == 0 else -1
                to = ((y + s * step[0]) % ny) * nz + (z + s * step[1]) % nz
                pairs.append(((y * nz + z) * nk + k, to * nk + k))
    return lax.ppermute(array, AXES, pairs)


def shifted(came, step):
    return [(y - step[0], z - step[1]) for y, z in came]


def spread(own):
    grid = (4, 8)
    steps = ((0, 2), (0, 4), (0, -2))
    four = jnp.concatenate([own] + [hop(own, grid, s) for s in steps], 0)
    came4 = [(0, 0)] + [shifted([(0, 0)], s)[0] for s in steps]
    far, left, right = (2, 0), (1, 1), (-1, 1)
    even = jnp.concatenate([four, hop(four, grid, far)], 0)
    came8 = came4 + shifted(came4, far)
    parts = [even, hop(four, grid, left), hop(four, grid, right), hop(even, grid, (1, 0)), hop(even, grid, (0, 1))]
    came = came8 + shifted(came4, left) + shifted(came4, right) + shifted(came8, (1, 0)) + shifted(came8, (0, 1))
    return parts, came


def shards(queries, keys, values, vertical):
    ctx = lax.axis_index("ctx")
    base = (ctx * TOK).astype(jnp.int32)[None]
    inner = jnp.zeros((1,), jnp.int32)
    first = (ctx == 0).astype(jnp.int32)[None]

    own, edge = pick(base, vertical, keys, values)
    edge = lax.ppermute(edge, "ctx", [(i, i + 1) for i in range(NCTX - 1)])
    parts, came = spread(own)

    sign = 1 - 2 * (lax.axis_index("kvh") % 2)
    oy = jnp.asarray([o[0] for o in came], jnp.int32)
    oz = jnp.asarray([o[1] for o in came], jnp.int32)
    device = ((ctx // 8 + sign * oy) % 4) * 8 + (ctx % 8 + sign * oz) % 8
    code = (device[:, None] * CAP + jnp.arange(CAP, dtype=jnp.int32)[None, :]).reshape(1, -1)

    acc1, ml1 = band(inner, queries, 1, keys, keys, values, values, 0, 1, 0, 1)
    acc0, ml0 = band(first, queries, 0, edge, keys, edge, values, 0, 0, 1, 0)
    return vert(base, queries, parts, vertical.T, code, acc0, ml0, acc1, ml1)


def solution(mesh):
    in_specs = (P("ctx", "kvh"), P("ctx", "kvh"), P("ctx", "kvh"), P("kvh", None))
    return jax.shard_map(shards, mesh=mesh, in_specs=in_specs, out_specs=P("ctx", "kvh"), check_vma=False)
```

```python
import math

import jax
import jax.numpy as jnp
from jax import lax
from jax.experimental import pallas as pl
from jax.experimental.pallas import tpu as pltpu
from jax.sharding import PartitionSpec as P

TOK = 2048
HEAD = 128
GROUP = 4
COLS = 512
BAND = 1024
CAP = 32
NCTX = 32
QB = 256
VR = HEAD + 16
C = math.log2(math.e) / math.sqrt(HEAD)
F32 = jnp.float32
BF = jnp.bfloat16
NEG = -1e30
LIMIT = 56 << 20
VERT_LIMIT = 56 << 20
PIECE = 512
QV = 512
TINY = 2.0**-60
HUGE = 2.0**100


def dot(a, b):
    return jnp.dot(a, b, preferred_element_type=F32)


def dot_t(a, b):
    return lax.dot_general(a, b, (((1,), (1,)), ((), ())), preferred_element_type=F32)


def pick_kernel(base_ref, vert_ref, k_ref, v_ref, out_ref, edge_ref):
    base = base_ref[0]
    vert = vert_ref[...]
    cols = lax.broadcasted_iota(jnp.int32, (CAP, COLS), 1)
    slot = lax.broadcasted_iota(jnp.int32, (CAP, COLS), 0)
    toks = lax.broadcasted_iota(jnp.int32, (CAP, TOK), 1)
    rows = []
    for h in range(GROUP):
        v = vert[h : h + 1, :] - base
        start = jnp.sum((v < 0).astype(jnp.int32), axis=1, keepdims=True)
        hit = (cols - start == slot) & (v < TOK)
        pos = jnp.sum(jnp.where(hit, v + 1, 0), axis=1, keepdims=True) - 1
        rows.append((toks == pos).astype(F32).astype(BF))
    sel = jnp.concatenate(rows, 0)
    out_ref[0, :, :HEAD] = dot(sel, k_ref[...]).astype(BF)
    out_ref[0, :, HEAD:] = dot(sel, v_ref[...]).astype(BF)
    edge_ref[:BAND, :] = k_ref[TOK - BAND :, :]
    edge_ref[BAND:, :] = v_ref[TOK - BAND :, :]


def pick(base, vertical, keys, values):
    full = lambda *s: pl.BlockSpec(s, lambda i: (0,) * len(s))
    return pl.pallas_call(
        pick_kernel,
        grid=(1,),
        out_shape=(
            jax.ShapeDtypeStruct((1, GROUP * CAP, 2 * HEAD), BF),
            jax.ShapeDtypeStruct((2 * BAND, HEAD), BF),
        ),
        in_specs=[pl.BlockSpec(memory_space=pltpu.SMEM), full(GROUP, COLS), full(TOK, HEAD), full(TOK, HEAD)],
        out_specs=(full(1, GROUP * CAP, 2 * HEAD), full(2 * BAND, HEAD)),
        compiler_params=pltpu.CompilerParams(vmem_limit_bytes=LIMIT),
        name="pick",
    )(base, vertical, keys, values)


def plan_kernel(came, place_ref, vert_ref, cols_ref, code_ref):
    place = place_ref[0]
    y, z, core = place >> 4, (place >> 1) & 7, place & 1
    wide = jnp.concatenate([vert_ref[...].astype(F32), jnp.zeros((8 - GROUP, COLS), F32)], 0)
    cols = wide.T.astype(jnp.int32)
    lanes = lax.broadcasted_iota(jnp.int32, (COLS, HEAD), 1)
    rows = lax.broadcasted_iota(jnp.int32, (COLS, 1), 0)
    lane8 = lax.broadcasted_iota(jnp.int32, (COLS, 8), 1)
    out = cols
    for h in range(GROUP):
        v = cols[:, h : h + 1]
        starts = jnp.sum((v < lanes * TOK).astype(jnp.int32), axis=0, keepdims=True)
        d = v >> 11
        start = jnp.sum(jnp.where(lanes == d, starts, 0), axis=1, keepdims=True)
        out = jnp.where(lane8 == GROUP + h, d * CAP + rows - start, out)
    cols_ref[...] = out
    slot = lax.broadcasted_iota(jnp.int32, (1, NCTX * CAP), 1)
    block, within = slot >> 5, slot & (CAP - 1)
    code = within
    for n, (a, b) in enumerate(zip(*came)):
        dy = jnp.where(core == 0, a[0], b[0])
        dz = jnp.where(core == 0, a[1], b[1])
        device = ((y + dy) & 3) * 8 + ((z + dz) & 7)
        code = jnp.where(block == n, within + device * CAP, code)
    code_ref[...] = code


def plan(came, place, vertical):
    full = lambda *s: pl.BlockSpec(s, lambda i: (0,) * len(s))
    return pl.pallas_call(
        lambda *refs: plan_kernel(came, *refs),
        grid=(1,),
        out_shape=(
            jax.ShapeDtypeStruct((COLS, 8), jnp.int32),
            jax.ShapeDtypeStruct((1, NCTX * CAP), jnp.int32),
        ),
        in_specs=[pl.BlockSpec(memory_space=pltpu.SMEM), full(GROUP, COLS)],
        out_specs=(full(COLS, 8), full(1, NCTX * CAP)),
        compiler_params=pltpu.CompilerParams(vmem_limit_bytes=LIMIT),
        name="plan",
    )(place, vertical)


def band_kernel(halo, blocks, first_ref, q_ref, *refs):
    own = blocks - halo
    k_refs, v_refs = list(refs[:own]), list(refs[own : 2 * own])
    if halo:
        edge = refs[2 * own]
        k_refs = [edge.at[pl.ds(BAND - (halo - n) * PIECE, PIECE)] for n in range(halo)] + k_refs
        v_refs = [edge.at[pl.ds(2 * BAND - (halo - n) * PIECE, PIECE)] for n in range(halo)] + v_refs
    acc_ref, ml_ref, kx, vt = refs[-4:]
    step = pl.program_id(0)

    @pl.when(step == 0)
    def _():
        first = first_ref[0] != 0
        for n, (k_ref, v_ref) in enumerate(zip(k_refs, v_refs)):
            at = slice(n * PIECE, (n + 1) * PIECE)
            k, v, one = k_ref[...], v_ref[...], jnp.ones((VR - HEAD, PIECE), BF)
            if n < halo:
                k = jnp.where(first, jnp.broadcast_to(k_refs[halo][0:1, :], k.shape), k)
                v = jnp.where(first, jnp.zeros_like(v), v)
                one = jnp.where(first, jnp.zeros_like(one), one)
            kx[at, :] = k
            vt[:HEAD, at] = v.T
            vt[HEAD:, at] = one

    off = pl.multiple_of(step * QB, QB)
    tri = lax.broadcasted_iota(jnp.int32, (QB, QB), 0) <= lax.broadcasted_iota(jnp.int32, (QB, QB), 1)

    def heads(exact):
        scores = lambda h: dot_t(kx[pl.ds(off, BAND + QB), :], q_ref[:, h * HEAD : (h + 1) * HEAD])
        nxt = scores(0)
        for h in range(GROUP):
            s = nxt
            if h + 1 < GROUP:
                nxt = scores(h + 1)
            s_in = s[QB:BAND]
            s_edge = jnp.where(tri, s[BAND:], s[:QB])
            m = jnp.zeros((1, QB), F32)
            if exact:
                m = jnp.maximum(jnp.max(s_in, axis=0, keepdims=True), jnp.max(s_edge, axis=0, keepdims=True))
                s_in, s_edge = s_in - m, s_edge - m
            p_in = jnp.exp2(s_in * C).astype(BF)
            p_edge = jnp.exp2(s_edge * C)
            p_last = jnp.where(tri, p_edge, 0.0).astype(BF)
            p_first = jnp.where(tri, 0.0, p_edge).astype(BF)
            p = jnp.concatenate([p_first, p_in, p_last], 0)
            o = dot(vt[:, pl.ds(off, BAND + QB)], p)
            acc_ref[h * HEAD : (h + 1) * HEAD, :] = o[:HEAD]
            ml_ref[h : h + 1, :] = m
            ml_ref[GROUP + h : GROUP + h + 1, :] = o[HEAD : HEAD + 1]

    heads(False)
    total = ml_ref[GROUP:, :]
    unsafe = jnp.max(jnp.where((total > TINY) & (total < HUGE), 0.0, 1.0)) > 0.0

    @pl.when(unsafe)
    def _():
        heads(True)


def band(piece, span, first, queries, edge, keys, values, before):
    n = span * PIECE // QB
    blocks = span + BAND // PIECE
    halo = max(BAND // PIECE - piece, 0)
    start = piece * PIECE // QB
    kv, specs = [], []
    for array in (keys, values):
        for b in range(max(piece - BAND // PIECE, 0), piece + span):
            kv.append(array)
            specs.append(pl.BlockSpec((PIECE, HEAD), lambda i, b=b: (b, 0)))
    if halo:
        kv.append(edge)
        specs.append(pl.BlockSpec(memory_space=pltpu.VMEM))
    return pl.pallas_call(
        lambda *refs: band_kernel(halo, blocks, *refs),
        grid=(n,),
        out_shape=(
            jax.ShapeDtypeStruct((GROUP * HEAD, TOK), F32),
            jax.ShapeDtypeStruct((2 * GROUP, TOK), F32),
        ),
        in_specs=[
            pl.BlockSpec(memory_space=pltpu.SMEM),
            pl.BlockSpec((QB, GROUP * HEAD), lambda i: (start + i, 0)),
            *specs,
            *[pl.BlockSpec(memory_space=pl.ANY)] * len(before),
        ],
        out_specs=(
            pl.BlockSpec((GROUP * HEAD, QB), lambda i: (0, start + i)),
            pl.BlockSpec((2 * GROUP, QB), lambda i: (0, start + i)),
        ),
        scratch_shapes=[pltpu.VMEM((blocks * PIECE, HEAD), BF), pltpu.VMEM((VR, blocks * PIECE), BF)],
        input_output_aliases={2 + len(kv) + i: i for i in range(len(before))},
        compiler_params=pltpu.CompilerParams(vmem_limit_bytes=LIMIT),
        cost_estimate=pl.CostEstimate(
            flops=8 * span * PIECE * GROUP * HEAD * (BAND + QB),
            bytes_accessed=3 << 20,
            transcendentals=span * PIECE * BAND * GROUP,
        ),
        name="band",
    )(first, queries, *kv, *before)


def vert_kernel(nparts, *refs):
    base_ref, q_ref = refs[:2]
    g_refs = refs[2 : 2 + nparts]
    cols_ref, code_ref, a_ref, ml_ref, out_ref, kx, vt = refs[2 + nparts :]
    step = pl.program_id(0)

    @pl.when(step == 0)
    def _():
        for h in range(GROUP):
            mine = cols_ref[:, GROUP + h : GROUP + h + 1]
            t = None
            at = 0
            for g in g_refs:
                n = g.shape[0] * CAP
                sel = (mine == code_ref[:, at : at + n]).astype(F32).astype(BF)
                at += n
                part = dot(sel, g[:, h * CAP : (h + 1) * CAP, :].reshape(n, 2 * HEAD))
                t = part if t is None else t + part
            kx[h] = t[:, :HEAD].astype(BF)
            vt[h, :HEAD, :] = t[:, HEAD:].astype(BF).T
            vt[h, HEAD:, :] = jnp.ones((VR - HEAD, COLS), BF)

    qpos = base_ref[0] + step * QV - BAND + lax.broadcasted_iota(jnp.int32, (1, QV), 1)

    def heads(exact):
        scores = lambda h: dot_t(kx[h], q_ref[:, h * HEAD : (h + 1) * HEAD])
        nxt = scores(0)
        top = jnp.zeros((1, QV), F32)
        for h in range(GROUP):
            s = nxt
            if h + 1 < GROUP:
                nxt = scores(h + 1)
            s = jnp.where(cols_ref[:, h : h + 1] <= qpos, s, NEG)
            a = a_ref[h * HEAD : (h + 1) * HEAD, :]
            lb = ml_ref[GROUP + h : GROUP + h + 1, :]
            if exact:
                mb = ml_ref[h : h + 1, :]
                m = jnp.maximum(jnp.max(s, axis=0, keepdims=True), mb)
                s = s - m
                alpha = jnp.exp2((mb - m) * C)
                a, lb = a * alpha, lb * alpha
            p = jnp.exp2(s * C).astype(BF)
            o = dot(vt[h], p)
            top = jnp.maximum(top, jnp.where(o[HEAD : HEAD + 1] < HUGE, 0.0, 1.0))
            den = o[HEAD : HEAD + 1] + lb
            out_ref[:, h * HEAD : (h + 1) * HEAD] = ((a + o[:HEAD]) * (1.0 / den)).T.astype(BF)
        return top

    top = heads(False)
    unsafe = jnp.max(jnp.maximum(top, jnp.max(jnp.abs(ml_ref[:GROUP, :]), axis=0, keepdims=True))) > 0.0

    @pl.when(unsafe)
    def _():
        heads(True)


def vert(base, queries, parts, cols, code, acc, ml):
    n = TOK // QV
    full = lambda *s: pl.BlockSpec(s, lambda i: (0,) * len(s))
    return pl.pallas_call(
        lambda *refs: vert_kernel(len(parts), *refs),
        grid=(n,),
        out_shape=jax.ShapeDtypeStruct((TOK, GROUP * HEAD), BF),
        in_specs=[
            pl.BlockSpec(memory_space=pltpu.SMEM),
            pl.BlockSpec((QV, GROUP * HEAD), lambda i: (i, 0)),
            *[pl.BlockSpec(memory_space=pltpu.VMEM)] * len(parts),
            full(COLS, 8),
            full(1, NCTX * CAP),
            pl.BlockSpec((GROUP * HEAD, QV), lambda i: (0, i)),
            pl.BlockSpec((2 * GROUP, QV), lambda i: (0, i)),
        ],
        out_specs=pl.BlockSpec((QV, GROUP * HEAD), lambda i: (i, 0)),
        scratch_shapes=[pltpu.VMEM((GROUP, COLS, HEAD), BF), pltpu.VMEM((GROUP, VR, COLS), BF)],
        compiler_params=pltpu.CompilerParams(vmem_limit_bytes=VERT_LIMIT),
        cost_estimate=pl.CostEstimate(
            flops=8 * TOK * GROUP * HEAD * COLS,
            bytes_accessed=12 << 20,
            transcendentals=TOK * COLS * GROUP,
        ),
        name="vert",
    )(base, queries, *parts, cols, code, acc, ml)


AXES = ("ctx", "kvh")


def hop(array, grid, steps):
    ny, nz = grid
    nk = lax.axis_size("kvh")
    pairs = []
    for y in range(ny):
        for z in range(nz):
            for k in range(nk):
                dy, dz = steps[k % 2]
                to = ((y + dy) % ny) * nz + (z + dz) % nz
                pairs.append(((y * nz + z) * nk + k, to * nk + k))
    return lax.ppermute(array, AXES, pairs)


def shifted(came, steps):
    return [[(y - dy, z - dz) for y, z in c] for c, (dy, dz) in zip(came, steps)]


def joined(*lists):
    return [sum((c[core] for c in lists), []) for core in range(2)]


ROUND1 = (((0, 2), (0, -2)), ((0, 4), (0, -4)), ((0, -2), (0, 2)))
FAR = ((2, 0), (-2, 0))
NEAR = (((1, 0), (-1, 0)), ((0, 1), (0, -1)), ((1, 1), (-1, -1)))


def order():
    here = [[(0, 0)], [(0, 0)]]
    four = joined(here, *[shifted(here, s) for s in ROUND1])
    even = joined(four, shifted(four, FAR))
    return joined(even, *[shifted(even, s) for s in NEAR])


def shards(queries, keys, values, vertical):
    ctx = lax.axis_index("ctx")
    base = (ctx * TOK).astype(jnp.int32)[None]
    first = (ctx == 0).astype(jnp.int32)[None]
    grid = (4, 8)
    after = lambda x, *waits: lax.optimization_barrier((x, *waits))[0]

    own, edge = pick(base, vertical, keys, values)
    got = [hop(own, grid, s) for s in ROUND1]
    place = (ctx * 2 + lax.axis_index("kvh") % 2).astype(jnp.int32)[None]
    slots = plan(order(), place, after(vertical, own))

    four = jnp.concatenate([own] + got, 0)
    four, slots, queries = lax.optimization_barrier((four, slots, queries))
    far = hop(four, grid, FAR)
    state = band(3, 1, first, queries, None, keys, values, ())

    edge, far, *state = lax.optimization_barrier((edge, far, *state))
    edge = lax.ppermute(edge, "ctx", [(i, i + 1) for i in range(NCTX - 1)])
    state = band(2, 1, first, queries, None, keys, values, state)

    even = jnp.concatenate([four, far], 0)
    even, *state = lax.optimization_barrier((even, *state))
    near = [hop(even, grid, s) for s in NEAR]
    state = band(0, 2, first, queries, edge, keys, values, state)
    return vert(base, queries, [even, *near], *slots, *state)


def solution(mesh):
    in_specs = (P("ctx", "kvh"), P("ctx", "kvh"), P("ctx", "kvh"), P("kvh", None))
    return jax.shard_map(shards, mesh=mesh, in_specs=in_specs, out_specs=P("ctx", "kvh"), check_vma=False)
```

```python
import math

import jax
import jax.numpy as jnp
from jax import lax
from jax.experimental import pallas as pl
from jax.experimental.pallas import tpu as pltpu
from jax.sharding import PartitionSpec as P

TOK = 2048
HEAD = 128
GROUP = 4
COLS = 512
BAND = 1024
CAP = 32
NCTX = 32
QB = 256
VR = HEAD + 16
C = math.log2(math.e) / math.sqrt(HEAD)
F32 = jnp.float32
BF = jnp.bfloat16
NEG = -1e30
LIMIT = 56 << 20
VERT_LIMIT = 56 << 20
PIECE = 512
QV = 512
TINY = 2.0**-60
HUGE = 2.0**100


def dot(a, b):
    return jnp.dot(a, b, preferred_element_type=F32)


def dot_t(a, b):
    return lax.dot_general(a, b, (((1,), (1,)), ((), ())), preferred_element_type=F32)


def pick_kernel(base_ref, vert_ref, k_ref, v_ref, out_ref, edge_ref):
    base = base_ref[0]
    vert = vert_ref[...]
    cols = lax.broadcasted_iota(jnp.int32, (CAP, COLS), 1)
    slot = lax.broadcasted_iota(jnp.int32, (CAP, COLS), 0)
    toks = lax.broadcasted_iota(jnp.int32, (CAP, TOK), 1)
    rows = []
    for h in range(GROUP):
        v = vert[h : h + 1, :] - base
        start = jnp.sum((v < 0).astype(jnp.int32), axis=1, keepdims=True)
        hit = (cols - start == slot) & (v < TOK)
        pos = jnp.sum(jnp.where(hit, v + 1, 0), axis=1, keepdims=True) - 1
        rows.append((toks == pos).astype(F32).astype(BF))
    sel = jnp.concatenate(rows, 0)
    out_ref[0, :, :HEAD] = dot(sel, k_ref[...]).astype(BF)
    out_ref[0, :, HEAD:] = dot(sel, v_ref[...]).astype(BF)
    edge_ref[:BAND, :] = k_ref[TOK - BAND :, :]
    edge_ref[BAND:, :] = v_ref[TOK - BAND :, :]


def pick(base, vertical, keys, values):
    full = lambda *s: pl.BlockSpec(s, lambda i: (0,) * len(s))
    return pl.pallas_call(
        pick_kernel,
        grid=(1,),
        out_shape=(
            jax.ShapeDtypeStruct((1, GROUP * CAP, 2 * HEAD), BF),
            jax.ShapeDtypeStruct((2 * BAND, HEAD), BF),
        ),
        in_specs=[pl.BlockSpec(memory_space=pltpu.SMEM), full(GROUP, COLS), full(TOK, HEAD), full(TOK, HEAD)],
        out_specs=(full(1, GROUP * CAP, 2 * HEAD), full(2 * BAND, HEAD)),
        compiler_params=pltpu.CompilerParams(vmem_limit_bytes=LIMIT),
        name="pick",
    )(base, vertical, keys, values)


def plan_kernel(came, place_ref, vert_ref, cols_ref, code_ref):
    place = place_ref[0]
    y, z, core = place >> 4, (place >> 1) & 7, place & 1
    wide = jnp.concatenate([vert_ref[...].astype(F32), jnp.zeros((8 - GROUP, COLS), F32)], 0)
    cols = wide.T.astype(jnp.int32)
    rows = lax.broadcasted_iota(jnp.int32, (COLS, 1), 0)
    lane8 = lax.broadcasted_iota(jnp.int32, (COLS, 8), 1)
    one = jnp.ones((COLS, HEAD), BF)
    out = cols
    for h in range(GROUP):
        d = cols[:, h : h + 1] >> 11
        earlier = ((vert_ref[h : h + 1, :] >> 11) < d).astype(F32).astype(BF)
        start = dot(earlier, one)[:, :8].astype(jnp.int32)
        out = jnp.where(lane8 == GROUP + h, d * CAP + rows - start, out)
    cols_ref[...] = out
    slot = lax.broadcasted_iota(jnp.int32, (1, NCTX * CAP), 1)
    block, within = slot >> 5, slot & (CAP - 1)
    code = within
    for n, (a, b) in enumerate(zip(*came)):
        dy = jnp.where(core == 0, a[0], b[0])
        dz = jnp.where(core == 0, a[1], b[1])
        device = ((y + dy) & 3) * 8 + ((z + dz) & 7)
        code = jnp.where(block == n, within + device * CAP, code)
    code_ref[...] = code


def plan(came, place, vertical):
    full = lambda *s: pl.BlockSpec(s, lambda i: (0,) * len(s))
    return pl.pallas_call(
        lambda *refs: plan_kernel(came, *refs),
        grid=(1,),
        out_shape=(
            jax.ShapeDtypeStruct((COLS, 8), jnp.int32),
            jax.ShapeDtypeStruct((1, NCTX * CAP), jnp.int32),
        ),
        in_specs=[pl.BlockSpec(memory_space=pltpu.SMEM), full(GROUP, COLS)],
        out_specs=(full(COLS, 8), full(1, NCTX * CAP)),
        compiler_params=pltpu.CompilerParams(vmem_limit_bytes=LIMIT),
        name="plan",
    )(place, vertical)


def band_kernel(halo, blocks, first_ref, q_ref, *refs):
    own = blocks - halo
    k_refs, v_refs = list(refs[:own]), list(refs[own : 2 * own])
    if halo:
        edge = refs[2 * own]
        k_refs = [edge.at[pl.ds(BAND - (halo - n) * PIECE, PIECE)] for n in range(halo)] + k_refs
        v_refs = [edge.at[pl.ds(2 * BAND - (halo - n) * PIECE, PIECE)] for n in range(halo)] + v_refs
    acc_ref, ml_ref, kx, vt = refs[-4:]
    step = pl.program_id(0)

    @pl.when(step == 0)
    def _():
        first = first_ref[0] != 0
        for n, (k_ref, v_ref) in enumerate(zip(k_refs, v_refs)):
            at = slice(n * PIECE, (n + 1) * PIECE)
            k, v, one = k_ref[...], v_ref[...], jnp.ones((VR - HEAD, PIECE), BF)
            if n < halo:
                k = jnp.where(first, jnp.broadcast_to(k_refs[halo][0:1, :], k.shape), k)
                v = jnp.where(first, jnp.zeros_like(v), v)
                one = jnp.where(first, jnp.zeros_like(one), one)
            kx[at, :] = k
            vt[:HEAD, at] = v.T
            vt[HEAD:, at] = one

    off = pl.multiple_of(step * QB, QB)
    tri = lax.broadcasted_iota(jnp.int32, (QB, QB), 0) <= lax.broadcasted_iota(jnp.int32, (QB, QB), 1)

    def heads(exact):
        scores = lambda h: dot_t(kx[pl.ds(off, BAND + QB), :], q_ref[:, h * HEAD : (h + 1) * HEAD])
        nxt = scores(0)
        for h in range(GROUP):
            s = nxt
            if h + 1 < GROUP:
                nxt = scores(h + 1)
            s_in = s[QB:BAND]
            s_edge = jnp.where(tri, s[BAND:], s[:QB])
            m = jnp.zeros((1, QB), F32)
            if exact:
                m = jnp.maximum(jnp.max(s_in, axis=0, keepdims=True), jnp.max(s_edge, axis=0, keepdims=True))
                s_in, s_edge = s_in - m, s_edge - m
            p_in = jnp.exp2(s_in * C).astype(BF)
            p_edge = jnp.exp2(s_edge * C)
            p_last = jnp.where(tri, p_edge, 0.0).astype(BF)
            p_first = jnp.where(tri, 0.0, p_edge).astype(BF)
            p = jnp.concatenate([p_first, p_in, p_last], 0)
            o = dot(vt[:, pl.ds(off, BAND + QB)], p)
            acc_ref[h * HEAD : (h + 1) * HEAD, :] = o[:HEAD]
            ml_ref[h : h + 1, :] = m
            ml_ref[GROUP + h : GROUP + h + 1, :] = o[HEAD : HEAD + 1]

    heads(False)
    total = ml_ref[GROUP:, :]
    unsafe = jnp.max(jnp.where((total > TINY) & (total < HUGE), 0.0, 1.0)) > 0.0

    @pl.when(unsafe)
    def _():
        heads(True)


def band(piece, span, first, queries, edge, keys, values, before):
    n = span * PIECE // QB
    blocks = span + BAND // PIECE
    halo = max(BAND // PIECE - piece, 0)
    start = piece * PIECE // QB
    kv, specs = [], []
    for array in (keys, values):
        for b in range(max(piece - BAND // PIECE, 0), piece + span):
            kv.append(array)
            specs.append(pl.BlockSpec((PIECE, HEAD), lambda i, b=b: (b, 0)))
    if halo:
        kv.append(edge)
        specs.append(pl.BlockSpec(memory_space=pltpu.VMEM))
    return pl.pallas_call(
        lambda *refs: band_kernel(halo, blocks, *refs),
        grid=(n,),
        out_shape=(
            jax.ShapeDtypeStruct((GROUP * HEAD, TOK), F32),
            jax.ShapeDtypeStruct((2 * GROUP, TOK), F32),
        ),
        in_specs=[
            pl.BlockSpec(memory_space=pltpu.SMEM),
            pl.BlockSpec((QB, GROUP * HEAD), lambda i: (start + i, 0)),
            *specs,
            *[pl.BlockSpec(memory_space=pl.ANY)] * len(before),
        ],
        out_specs=(
            pl.BlockSpec((GROUP * HEAD, QB), lambda i: (0, start + i)),
            pl.BlockSpec((2 * GROUP, QB), lambda i: (0, start + i)),
        ),
        scratch_shapes=[pltpu.VMEM((blocks * PIECE, HEAD), BF), pltpu.VMEM((VR, blocks * PIECE), BF)],
        input_output_aliases={2 + len(kv) + i: i for i in range(len(before))},
        compiler_params=pltpu.CompilerParams(vmem_limit_bytes=LIMIT),
        cost_estimate=pl.CostEstimate(
            flops=8 * span * PIECE * GROUP * HEAD * (BAND + QB),
            bytes_accessed=3 << 20,
            transcendentals=span * PIECE * BAND * GROUP,
        ),
        name="band",
    )(first, queries, *kv, *before)


def vert_kernel(nparts, *refs):
    base_ref, q_ref = refs[:2]
    g_refs = refs[2 : 2 + nparts]
    cols_ref, code_ref, a_ref, ml_ref, out_ref, kx, vt = refs[2 + nparts :]
    step = pl.program_id(0)

    @pl.when(step == 0)
    def _():
        for h in range(GROUP):
            mine = cols_ref[:, GROUP + h : GROUP + h + 1]
            t = None
            at = 0
            for g in g_refs:
                n = g.shape[0] * CAP
                sel = (mine == code_ref[:, at : at + n]).astype(F32).astype(BF)
                at += n
                part = dot(sel, g[:, h * CAP : (h + 1) * CAP, :].reshape(n, 2 * HEAD))
                t = part if t is None else t + part
            kx[h] = t[:, :HEAD].astype(BF)
            vt[h, :HEAD, :] = t[:, HEAD:].astype(BF).T
            vt[h, HEAD:, :] = jnp.ones((VR - HEAD, COLS), BF)

    qpos = base_ref[0] + step * QV - BAND + lax.broadcasted_iota(jnp.int32, (1, QV), 1)

    def heads(exact):
        scores = lambda h: dot_t(kx[h], q_ref[:, h * HEAD : (h + 1) * HEAD])
        nxt = scores(0)
        top = jnp.zeros((1, QV), F32)
        for h in range(GROUP):
            s = nxt
            if h + 1 < GROUP:
                nxt = scores(h + 1)
            s = jnp.where(cols_ref[:, h : h + 1] <= qpos, s, NEG)
            a = a_ref[h * HEAD : (h + 1) * HEAD, :]
            lb = ml_ref[GROUP + h : GROUP + h + 1, :]
            if exact:
                mb = ml_ref[h : h + 1, :]
                m = jnp.maximum(jnp.max(s, axis=0, keepdims=True), mb)
                s = s - m
                alpha = jnp.exp2((mb - m) * C)
                a, lb = a * alpha, lb * alpha
            p = jnp.exp2(s * C).astype(BF)
            o = dot(vt[h], p)
            top = jnp.maximum(top, jnp.where(o[HEAD : HEAD + 1] < HUGE, 0.0, 1.0))
            den = o[HEAD : HEAD + 1] + lb
            out_ref[:, h * HEAD : (h + 1) * HEAD] = ((a + o[:HEAD]) * (1.0 / den)).T.astype(BF)
        return top

    top = heads(False)
    unsafe = jnp.max(jnp.maximum(top, jnp.max(jnp.abs(ml_ref[:GROUP, :]), axis=0, keepdims=True))) > 0.0

    @pl.when(unsafe)
    def _():
        heads(True)


def vert(base, queries, parts, cols, code, acc, ml):
    n = TOK // QV
    full = lambda *s: pl.BlockSpec(s, lambda i: (0,) * len(s))
    return pl.pallas_call(
        lambda *refs: vert_kernel(len(parts), *refs),
        grid=(n,),
        out_shape=jax.ShapeDtypeStruct((TOK, GROUP * HEAD), BF),
        in_specs=[
            pl.BlockSpec(memory_space=pltpu.SMEM),
            pl.BlockSpec((QV, GROUP * HEAD), lambda i: (i, 0)),
            *[pl.BlockSpec(memory_space=pltpu.VMEM)] * len(parts),
            full(COLS, 8),
            full(1, NCTX * CAP),
            pl.BlockSpec((GROUP * HEAD, QV), lambda i: (0, i)),
            pl.BlockSpec((2 * GROUP, QV), lambda i: (0, i)),
        ],
        out_specs=pl.BlockSpec((QV, GROUP * HEAD), lambda i: (i, 0)),
        scratch_shapes=[pltpu.VMEM((GROUP, COLS, HEAD), BF), pltpu.VMEM((GROUP, VR, COLS), BF)],
        compiler_params=pltpu.CompilerParams(vmem_limit_bytes=VERT_LIMIT),
        cost_estimate=pl.CostEstimate(
            flops=8 * TOK * GROUP * HEAD * COLS,
            bytes_accessed=12 << 20,
            transcendentals=TOK * COLS * GROUP,
        ),
        name="vert",
    )(base, queries, *parts, cols, code, acc, ml)


AXES = ("ctx", "kvh")


def hop(array, grid, steps):
    ny, nz = grid
    nk = lax.axis_size("kvh")
    pairs = []
    for y in range(ny):
        for z in range(nz):
            for k in range(nk):
                dy, dz = steps[k % 2]
                to = ((y + dy) % ny) * nz + (z + dz) % nz
                pairs.append(((y * nz + z) * nk + k, to * nk + k))
    return lax.ppermute(array, AXES, pairs)


def shifted(came, steps):
    return [[(y - dy, z - dz) for y, z in c] for c, (dy, dz) in zip(came, steps)]


def joined(*lists):
    return [sum((c[core] for c in lists), []) for core in range(2)]


ROUND1 = (((0, 2), (0, -2)), ((0, 4), (0, -4)), ((0, -2), (0, 2)))
FAR = ((2, 0), (-2, 0))
NEAR = (((1, 0), (-1, 0)), ((0, 1), (0, -1)), ((1, 1), (-1, -1)))


def order():
    here = [[(0, 0)], [(0, 0)]]
    four = joined(here, *[shifted(here, s) for s in ROUND1])
    even = joined(four, shifted(four, FAR))
    return joined(even, *[shifted(even, s) for s in NEAR])


def shards(queries, keys, values, vertical):
    ctx = lax.axis_index("ctx")
    base = (ctx * TOK).astype(jnp.int32)[None]
    first = (ctx == 0).astype(jnp.int32)[None]
    grid = (4, 8)
    after = lambda x, *waits: lax.optimization_barrier((x, *waits))[0]

    own, edge = pick(base, vertical, keys, values)
    got = [hop(own, grid, s) for s in ROUND1]
    place = (ctx * 2 + lax.axis_index("kvh") % 2).astype(jnp.int32)[None]

    four = jnp.concatenate([own] + got, 0)
    four, queries = lax.optimization_barrier((four, queries))
    far = hop(four, grid, FAR)
    slots = plan(order(), place, after(vertical, four))
    edge, slots = lax.optimization_barrier((edge, slots))
    edge = lax.ppermute(edge, "ctx", [(i, i + 1) for i in range(NCTX - 1)])
    state = band(2, 2, first, after(queries, slots[0]), None, keys, values, ())

    even = jnp.concatenate([four, far], 0)
    even, *state = lax.optimization_barrier((even, *state))
    near = [hop(even, grid, s) for s in NEAR]
    state = band(0, 2, first, queries, edge, keys, values, state)
    return vert(base, queries, [even, *near], *slots, *state)


def solution(mesh):
    in_specs = (P("ctx", "kvh"), P("ctx", "kvh"), P("ctx", "kvh"), P("kvh", None))
    return jax.shard_map(shards, mesh=mesh, in_specs=in_specs, out_specs=P("ctx", "kvh"), check_vma=False)
```
